32 devices in a mesh: curve: 8 (over z, y), sub: 4 (over x, core).
Axes of the slice: x: 2, y: 2, z: 4, core: 2. Of those that a mesh axis runs over, the one named last changes fastest.
Arguments:
- densities: bfloat16 [192, 16384], P(None, ('curve', 'sub')), may hold values from -6 to 6
- far_lists: int32 [200, 16384], P(None, ('curve', 'sub')), may hold values from 0 to 1536
- near_lists: int32 [26, 16384], P(None, ('curve', 'sub')), may hold values from 0 to 1535
- ghost_sends: int32 [32768], P(('curve', 'sub')), may hold values from 0 to 511
- top_lists: int32 [200, 32], P(None, ('curve', 'sub')), may hold values from 0 to 32
- point_to_mult: bfloat16 [32256], replicated, may hold values from -0.4375 to 0.4375
- mult_to_mult: bfloat16 [225792], replicated, may hold values from -0.15625 to 0.15625
- mult_to_local: bfloat16 [5644800], replicated, may hold values from -0.03125 to 0.03125
- local_to_local: bfloat16 [225792], replicated, may hold values from -0.5 to 0.5
- local_to_point: bfloat16 [32256], replicated, may hold values from -0.5 to 0.5
- point_to_point: bfloat16 [995328], replicated, may hold values from -0.078125 to 0.078125
Outputs:
- velocity: float32 [192, 16384], P(None, ('curve', 'sub'))
The draws below stay inside these ranges and needn't reach their ends.
Inputs may be any that keep to these rules, and one draw needn't show every extreme that they name: `far_lists`: an entry equal to 1536 marks an absent interaction. `ghost_sends`: entries are leaf indices local to the sending device. `top_lists`: an entry equal to 32 marks an absent interaction.
All inputs are finite; a program needn't handle non-finite values.
Results may differ from the reference program's by a relative error of at most 0.0085.
Values may be sent and summed in bfloat16 or wider, within the bound.
A program may use at most 192 MiB of HBM per device.

```python
import jax
import jax.numpy as jnp
from jax import lax

OFFSETS = 200
NEAR = 26
LEVELS = 3
EW = 168
DW = 192
LEAF_DEV = 512
GHOST = 32
NLEAF = 16384
NBOX = 32
N_CURVE = 8
N_SUB = 4
DEVICES = 32


def plant(values, stream_key, least, largest):
    index_at = [jax.random.randint(jax.random.fold_in(stream_key, axis), (), 0, length) for axis, length in enumerate(values.shape)]
    main_axis = values.shape.index(max(values.shape))
    next_to = index_at[:main_axis] + [(index_at[main_axis] + 1) % values.shape[main_axis]] + index_at[main_axis + 1:]
    return values.at[tuple(index_at)].set(least).at[tuple(next_to)].set(largest)


def block_levels(rng, extent, pieces, smallest, top_value):
    def one(axis_at, shards_of):
        heights = jax.random.uniform(jax.random.fold_in(jax.random.fold_in(rng, 6), axis_at), (shards_of,), jnp.float32, smallest / len(pieces), top_value / len(pieces))
        return jnp.repeat(jnp.exp(heights), extent[axis_at] // shards_of).reshape((-1,) + (1,) * (len(extent) - axis_at - 1))

    factor_of = one(*pieces[0])
    for cut in pieces[1:]:
        factor_of = factor_of * one(*cut)
    return factor_of


def scatter_about(stream_key, dims, deviation, bound, shards=(), held_as=jnp.bfloat16):
    values = jax.random.normal(stream_key, dims, jnp.float32) * deviation
    if len(shards) > 0:
        values = block_levels(stream_key, dims, shards, -0.22, 0.18) * values
    return jnp.clip(values, min=-bound, max=bound).astype(held_as)


def setup_inputs(seed: int = 0) -> dict:
    key_of = jax.random.split(jax.random.key(seed), 12)
    densities = scatter_about(key_of[0], (DW, NLEAF), 1.0, 6.0, ((1, 32),))
    far_lists = plant(jax.random.randint(key_of[1], (OFFSETS, NLEAF), 0, LEAF_DEV + DEVICES * GHOST + 1), jax.random.fold_in(key_of[1], 1), 0, LEAF_DEV + DEVICES * GHOST).astype(jnp.int32)
    near_lists = plant(jax.random.randint(key_of[2], (NEAR, NLEAF), 0, LEAF_DEV + DEVICES * GHOST), jax.random.fold_in(key_of[2], 1), 0, (LEAF_DEV + DEVICES * GHOST) - 1).astype(jnp.int32)
    ghost_sends = plant(jax.random.randint(key_of[3], (DEVICES * DEVICES * GHOST,), 0, LEAF_DEV), jax.random.fold_in(key_of[3], 1), 0, LEAF_DEV - 1).astype(jnp.int32)
    top_lists = plant(jax.random.randint(key_of[4], (OFFSETS, NBOX), 0, NBOX + 1), jax.random.fold_in(key_of[4], 1), 0, NBOX).astype(jnp.int32)
    point_to_mult = scatter_about(key_of[5], (DW * EW,), DW ** -0.5, 0.4375)
    mult_to_mult = scatter_about(key_of[6], (8 * EW * EW,), (8 * EW) ** -0.5, 0.15625)
    mult_to_local = scatter_about(key_of[7], (OFFSETS * EW * EW,), (OFFSETS * EW) ** -0.5, 0.03125)
    local_to_local = scatter_about(key_of[8], (8 * EW * EW,), EW ** -0.5, 0.5)
    local_to_point = scatter_about(key_of[9], (EW * DW,), EW ** -0.5, 0.5)
    point_to_point = scatter_about(key_of[10], ((NEAR + 1) * DW * DW,), ((NEAR + 1) * DW) ** -0.5, 0.078125)
    return {"densities": densities, "far_lists": far_lists, "near_lists": near_lists, "ghost_sends": ghost_sends, "top_lists": top_lists, "point_to_mult": point_to_mult, "mult_to_mult": mult_to_mult, "mult_to_local": mult_to_local, "local_to_local": local_to_local, "local_to_point": local_to_point, "point_to_point": point_to_point}


def reference(densities, far_lists, near_lists, ghost_sends, top_lists, point_to_mult, mult_to_mult, mult_to_local, local_to_local, local_to_point, point_to_point):
    dev_count = N_CURVE * N_SUB
    p2m = point_to_mult.reshape(DW, EW).astype(jnp.float32)
    m2m = mult_to_mult.reshape(8, EW, EW).astype(jnp.float32)
    m2l = mult_to_local.reshape(OFFSETS, EW, EW).astype(jnp.float32)
    l2l = local_to_local.reshape(8, EW, EW).astype(jnp.float32)
    l2p = local_to_point.reshape(EW, DW).astype(jnp.float32)
    p2p = point_to_point.reshape(NEAR + 1, DW, DW).astype(jnp.float32)
    mult_zero = jnp.einsum("dl,de->el", densities.astype(jnp.float32), p2m).astype(jnp.bfloat16)
    level_mult = mult_zero
    for level_index in range(LEVELS):
        grouped = level_mult.astype(jnp.float32).reshape(EW, -1, 8)
        level_mult = jnp.einsum("ebk,kef->fb", grouped, m2m).astype(jnp.bfloat16)
    top_pool = jnp.concatenate([level_mult, jnp.zeros((EW, 1), jnp.bfloat16)], axis=1)
    picked = top_pool[:, top_lists].astype(jnp.float32)
    local_exp = jnp.einsum("ecb,cef->fb", picked, m2l).astype(jnp.bfloat16)
    leaf_far = None
    for level_index in range(LEVELS):
        child_exp = jnp.einsum("eb,kef->fbk", local_exp.astype(jnp.float32), l2l).reshape(EW, -1)
        if level_index < LEVELS - 1:
            local_exp = child_exp.astype(jnp.bfloat16)
        else:
            leaf_far = child_exp
    sends = ghost_sends.reshape(dev_count, dev_count, GHOST)
    owners = jnp.arange(dev_count, dtype=jnp.int32)
    ghost_map = (owners[:, None, None] * LEAF_DEV + sends).transpose(1, 0, 2).reshape(dev_count, dev_count * GHOST)
    local_map = owners[:, None] * LEAF_DEV + jnp.arange(LEAF_DEV, dtype=jnp.int32)[None, :]
    global_map = jnp.concatenate([local_map, ghost_map, jnp.full((dev_count, 1), NLEAF, jnp.int32)], axis=1).astype(jnp.int32)
    mult_pool = jnp.concatenate([mult_zero, jnp.zeros((EW, 1), jnp.bfloat16)], axis=1)
    dens_pool = jnp.concatenate([densities, jnp.zeros((DW, 1), jnp.bfloat16)], axis=1)

    def per_device(device):
        begin = (device * LEAF_DEV).astype(jnp.int32)
        mapping = global_map[device]
        far_idx = mapping[lax.dynamic_slice_in_dim(far_lists, begin, LEAF_DEV, 1)]
        near_idx = mapping[lax.dynamic_slice_in_dim(near_lists, begin, LEAF_DEV, 1)]
        own_dens = lax.dynamic_slice_in_dim(densities, begin, LEAF_DEV, 1).astype(jnp.float32)
        own_far = lax.dynamic_slice_in_dim(leaf_far, begin, LEAF_DEV, 1)
        gathered = mult_pool[:, far_idx].astype(jnp.float32)
        leaf_local = (own_far + jnp.einsum("ecl,cef->fl", gathered, m2l)).astype(jnp.bfloat16)
        far_vel = jnp.einsum("el,ed->dl", leaf_local.astype(jnp.float32), l2p)
        neighbours = dens_pool[:, near_idx].astype(jnp.float32)
        near_vel = jnp.einsum("dcl,cdf->fl", neighbours, p2p[:NEAR]) + jnp.einsum("dl,df->fl", own_dens, p2p[NEAR])
        return far_vel + near_vel

    result = lax.map(per_device, jnp.arange(dev_count, dtype=jnp.int32))
    return result.transpose(1, 0, 2).reshape(DW, -1)
```

```python
import jax
import jax.numpy as jnp
from jax import lax
from jax.experimental import pallas as pl
from jax.experimental.pallas import tpu as pltpu
from jax.sharding import PartitionSpec as P

LEVELS = 3
BLOCK = 8
BF = jnp.bfloat16
F32 = jnp.float32


def one_hot(row, depth):
    shape = (depth, row.shape[1])
    key = jnp.broadcast_to(row.astype(jnp.int16), shape)
    ids = lax.broadcasted_iota(jnp.int16, shape, 0)
    return jnp.where(key == ids, jnp.ones(shape, BF), jnp.zeros(shape, BF))


def dot_t(left, right):
    return lax.dot_general(left, right, (((0,), (0,)), ((), ())), preferred_element_type=F32)


def far_kernel(lists, m2l, pool, top, far, top_far, picked):
    ewidth, depth = pool.shape

    @pl.when(pl.program_id(0) == 0)
    def _():
        far[...] = jnp.zeros_like(far)
        top_far[...] = jnp.zeros_like(top_far)

    @pl.loop(0, BLOCK // 2)
    def _(pair):
        both = []
        for half in range(2):
            hot = one_hot(lists[pl.ds(2 * pair + half, 1), :], depth)
            both.append(jnp.dot(pool[...], hot, preferred_element_type=F32))
        start = pl.multiple_of(pair * (2 * ewidth), 16)
        picked[pl.ds(start, 2 * ewidth), :] = jnp.concatenate(both, axis=0).astype(BF)

    far[...] += dot_t(m2l[...], picked[...])
    top_far[...] += jnp.dot(top[0], m2l[...], preferred_element_type=F32)


def far_call(far_lists, m2l_rows, pool, top):
    offsets, leaves = far_lists.shape
    ewidth, depth = pool.shape
    rows = BLOCK * ewidth
    return pl.pallas_call(
        far_kernel,
        grid=(offsets // BLOCK,),
        in_specs=[
            pl.BlockSpec((BLOCK, leaves), lambda i: (i, 0)),
            pl.BlockSpec((rows, ewidth), lambda i: (i, 0)),
            pl.BlockSpec((ewidth, depth), lambda i: (0, 0)),
            pl.BlockSpec((1, 1, rows), lambda i: (i, 0, 0)),
        ],
        out_specs=[
            pl.BlockSpec((ewidth, leaves), lambda i: (0, 0)),
            pl.BlockSpec((1, ewidth), lambda i: (0, 0)),
        ],
        out_shape=[
            jax.ShapeDtypeStruct((ewidth, leaves), F32),
            jax.ShapeDtypeStruct((1, ewidth), F32),
        ],
        scratch_shapes=[pltpu.VMEM((rows, leaves), BF)],
        compiler_params=pltpu.CompilerParams(vmem_limit_bytes=48 * 2**20),
    )(far_lists, m2l_rows, pool, top)


def near_kernel(lists, p2p, pool, out, picked):
    dwidth, depth = pool.shape
    classes, leaves = lists.shape

    @pl.loop(0, classes)
    def _(c):
        hot = one_hot(lists[pl.ds(c, 1), :], depth)
        found = jnp.dot(pool[...], hot, preferred_element_type=F32).astype(BF)
        picked[pl.ds(pl.multiple_of(c * dwidth, 16), dwidth), :] = found

    picked[classes * dwidth :, :] = pool[:, :leaves]
    out[...] = dot_t(p2p[...], picked[...])


def near_call(near_lists, p2p_rows, pool):
    classes, leaves = near_lists.shape
    dwidth, depth = pool.shape
    return pl.pallas_call(
        near_kernel,
        out_shape=jax.ShapeDtypeStruct((dwidth, leaves), F32),
        scratch_shapes=[pltpu.VMEM(((classes + 1) * dwidth, leaves), BF)],
        compiler_params=pltpu.CompilerParams(vmem_limit_bytes=48 * 2**20),
    )(near_lists, p2p_rows, pool)


def shards(
    densities,
    far_lists,
    near_lists,
    ghost_sends,
    top_lists,
    point_to_mult,
    mult_to_mult,
    mult_to_local,
    local_to_local,
    local_to_point,
    point_to_point,
):
    axes = ("curve", "sub")
    devices = lax.axis_size(axes)
    dwidth, leaf_count = densities.shape
    offset_count = far_lists.shape[0]
    near_count = near_lists.shape[0]
    ewidth = point_to_mult.shape[0] // dwidth
    p2m = point_to_mult.reshape(dwidth, ewidth)
    m2m = mult_to_mult.reshape(8, ewidth, ewidth)
    m2l_rows = mult_to_local.reshape(offset_count * ewidth, ewidth)
    l2l = local_to_local.reshape(8, ewidth, ewidth)
    l2p = local_to_point.reshape(ewidth, dwidth)
    p2p_rows = point_to_point.reshape((near_count + 1) * dwidth, dwidth)

    sends = ghost_sends[:, None] == lax.broadcasted_iota(jnp.int32, (1, leaf_count), 1)
    packed = lax.dot_general(
        sends.astype(BF), densities, (((1,), (1,)), ((), ())), preferred_element_type=F32
    ).astype(BF)
    arrived = lax.all_to_all(packed, axes, split_axis=0, concat_axis=0, tiled=True)

    mult_rows = jnp.einsum("dl,de->le", densities, p2m, preferred_element_type=F32).astype(BF)
    level_mult = mult_rows.T
    for level_index in range(LEVELS):
        grouped = level_mult.reshape(ewidth, -1, 8)
        level_mult = jnp.einsum("ebk,kef->fb", grouped, m2m, preferred_element_type=F32).astype(BF)
    mine = level_mult.T
    copies = jnp.broadcast_to(mine[None], (devices,) + mine.shape)
    top_boxes = lax.all_to_all(copies, axes, split_axis=0, concat_axis=0, tiled=True)
    top_boxes = top_boxes.reshape(-1, ewidth)
    top_hot = top_lists == lax.broadcasted_iota(jnp.int32, (1, top_boxes.shape[0]), 1)
    top_picked = jnp.dot(top_hot.astype(BF), top_boxes, preferred_element_type=F32).astype(BF)

    dens_pool = jnp.concatenate([densities, arrived.T], axis=1)
    mult_pool = jnp.einsum("dl,de->el", dens_pool, p2m, preferred_element_type=F32).astype(BF)
    far, top_far = far_call(
        far_lists,
        m2l_rows,
        mult_pool,
        top_picked.reshape(offset_count // BLOCK, 1, BLOCK * ewidth),
    )
    near = near_call(near_lists, p2p_rows, dens_pool)

    local_exp = top_far.T.astype(BF)
    leaf_far = None
    for level_index in range(LEVELS):
        child_exp = jnp.einsum(
            "eb,kef->fbk", local_exp, l2l, preferred_element_type=F32
        ).reshape(ewidth, -1)
        if level_index < LEVELS - 1:
            local_exp = child_exp.astype(BF)
        else:
            leaf_far = child_exp
    leaf_local = (leaf_far + far).astype(BF)
    return near + jnp.einsum("el,ed->dl", leaf_local, l2p, preferred_element_type=F32)


def solution(mesh):
    in_specs = (
        P(None, ("curve", "sub")),
        P(None, ("curve", "sub")),
        P(None, ("curve", "sub")),
        P(("curve", "sub")),
        P(None, ("curve", "sub")),
        P(),
        P(),
        P(),
        P(),
        P(),
        P(),
    )
    out_specs = P(None, ("curve", "sub"))
    return jax.shard_map(shards, mesh=mesh, in_specs=in_specs, out_specs=out_specs, check_vma=False)
```

```python
import functools
import math

import jax
import jax.numpy as jnp
from jax import lax
from jax.experimental import pallas as pl
from jax.experimental.pallas import tpu as pltpu
from jax.sharding import PartitionSpec as P

LEVELS = 3
BLOCK = 8
BF = jnp.bfloat16
F32 = jnp.float32


def one_hot(row, depth):
    shape = (depth, row.shape[1])
    key = jnp.broadcast_to(row.astype(jnp.int16), shape)
    ids = lax.broadcasted_iota(jnp.int16, shape, 0)
    return jnp.where(key == ids, jnp.ones(shape, BF), jnp.zeros(shape, BF))


def dot_t(left, right):
    return lax.dot_general(left, right, (((0,), (0,)), ((), ())), preferred_element_type=F32)


def rows_kernel(width, period, lanes, flat, out, wide, placed):
    groups = wide.shape[0] // lanes
    wide[...] = flat[...].astype(F32)

    def line(at):
        return wide[pl.ds(at, groups, stride=lanes), :]

    for row in range(period):
        start, offset = divmod(row * width, 128)
        for low in range(0, width, 128):
            size = min(128, width - low)
            here = start + low // 128
            first = line(here)
            if offset:
                rest = line(here + 1) if offset + size > 128 else first
                first = jnp.concatenate([first[:, offset:], rest[:, :offset]], axis=1)
            placed[low // 128, pl.ds(row, groups, stride=period), :] = first
    for low in range(0, width, 128):
        high = min(low + 128, width)
        out[:, low:high] = placed[low // 128, :, : high - low].astype(BF)


def as_rows(flat, width, groups):
    total = flat.shape[0]
    period = 128 // math.gcd(width, 128)
    lanes = width * period // 128
    return pl.pallas_call(
        functools.partial(rows_kernel, width, period, lanes),
        grid=(pl.cdiv(total // (width * period), groups),),
        in_specs=[pl.BlockSpec((groups * lanes, 128), lambda i: (i, 0))],
        out_specs=pl.BlockSpec((groups * period, width), lambda i: (i, 0)),
        out_shape=jax.ShapeDtypeStruct((total // width, width), BF),
        scratch_shapes=[
            pltpu.VMEM((groups * lanes, 128), F32),
            pltpu.VMEM((pl.cdiv(width, 128), groups * period, 128), F32),
        ],
        compiler_params=pltpu.CompilerParams(vmem_limit_bytes=48 * 2**20),
    )(flat.reshape(total // 128, 128))


def far_kernel(lists, m2l, pool, top, far, top_far, picked):
    ewidth, depth = pool.shape

    @pl.when(pl.program_id(0) == 0)
    def _():
        far[...] = jnp.zeros_like(far)
        top_far[...] = jnp.zeros_like(top_far)

    @pl.loop(0, BLOCK // 2)
    def _(pair):
        both = []
        for half in range(2):
            hot = one_hot(lists[pl.ds(2 * pair + half, 1), :], depth)
            both.append(jnp.dot(pool[...], hot, preferred_element_type=F32))
        start = pl.multiple_of(pair * (2 * ewidth), 16)
        picked[pl.ds(start, 2 * ewidth), :] = jnp.concatenate(both, axis=0).astype(BF)

    far[...] += dot_t(m2l[...], picked[...])
    top_far[...] += jnp.dot(top[0], m2l[...], preferred_element_type=F32)


def far_call(far_lists, m2l_rows, pool, top):
    offsets, leaves = far_lists.shape
    ewidth, depth = pool.shape
    rows = BLOCK * ewidth
    return pl.pallas_call(
        far_kernel,
        grid=(offsets // BLOCK,),
        in_specs=[
            pl.BlockSpec((BLOCK, leaves), lambda i: (i, 0)),
            pl.BlockSpec((rows, ewidth), lambda i: (i, 0)),
            pl.BlockSpec((ewidth, depth), lambda i: (0, 0)),
            pl.BlockSpec((1, 1, rows), lambda i: (i, 0, 0)),
        ],
        out_specs=[
            pl.BlockSpec((ewidth, leaves), lambda i: (0, 0)),
            pl.BlockSpec((1, ewidth), lambda i: (0, 0)),
        ],
        out_shape=[
            jax.ShapeDtypeStruct((ewidth, leaves), F32),
            jax.ShapeDtypeStruct((1, ewidth), F32),
        ],
        scratch_shapes=[pltpu.VMEM((rows, leaves), BF)],
        compiler_params=pltpu.CompilerParams(vmem_limit_bytes=48 * 2**20),
    )(far_lists, m2l_rows, pool, top)


def near_kernel(lists, p2p, pool, out, picked):
    dwidth, depth = pool.shape
    classes, leaves = lists.shape

    @pl.loop(0, classes)
    def _(c):
        hot = one_hot(lists[pl.ds(c, 1), :], depth)
        found = jnp.dot(pool[...], hot, preferred_element_type=F32).astype(BF)
        picked[pl.ds(pl.multiple_of(c * dwidth, 16), dwidth), :] = found

    picked[classes * dwidth :, :] = pool[:, :leaves]
    out[...] = dot_t(p2p[...], picked[...])


def near_call(near_lists, p2p_rows, pool):
    classes, leaves = near_lists.shape
    dwidth, depth = pool.shape
    return pl.pallas_call(
        near_kernel,
        out_shape=jax.ShapeDtypeStruct((dwidth, leaves), F32),
        scratch_shapes=[pltpu.VMEM(((classes + 1) * dwidth, leaves), BF)],
        compiler_params=pltpu.CompilerParams(vmem_limit_bytes=48 * 2**20),
    )(near_lists, p2p_rows, pool)


def shards(
    densities,
    far_lists,
    near_lists,
    ghost_sends,
    top_lists,
    point_to_mult,
    mult_to_mult,
    mult_to_local,
    local_to_local,
    local_to_point,
    point_to_point,
):
    axes = ("curve", "sub")
    devices = lax.axis_size(axes)
    dwidth, leaf_count = densities.shape
    offset_count = far_lists.shape[0]
    near_count = near_lists.shape[0]
    ewidth = point_to_mult.shape[0] // dwidth
    p2m = point_to_mult.reshape(dwidth, ewidth)
    m2m = as_rows(mult_to_mult, ewidth, 48).reshape(8, ewidth, ewidth)
    m2l_rows = as_rows(mult_to_local, ewidth, 240)
    l2l = as_rows(local_to_local, ewidth, 48).reshape(8, ewidth, ewidth)
    l2p = local_to_point.reshape(ewidth, dwidth)
    p2p_rows = as_rows(point_to_point, dwidth, 864)

    sends = ghost_sends[:, None] == lax.broadcasted_iota(jnp.int32, (1, leaf_count), 1)
    packed = lax.dot_general(
        sends.astype(BF), densities, (((1,), (1,)), ((), ())), preferred_element_type=F32
    ).astype(BF)
    mult_rows = jnp.einsum("dl,de->le", densities, p2m, preferred_element_type=F32).astype(BF)
    level_mult = mult_rows.T
    for level_index in range(LEVELS):
        grouped = level_mult.reshape(ewidth, -1, 8)
        level_mult = jnp.einsum("ebk,kef->fb", grouped, m2m, preferred_element_type=F32).astype(BF)
    ghosts = ghost_sends.shape[0] // devices
    tops = jnp.pad(level_mult.T, ((0, 0), (0, dwidth - ewidth)))
    tops = jnp.broadcast_to(tops[None], (devices,) + tops.shape)
    leaving = jnp.concatenate([packed.reshape(devices, ghosts, dwidth), tops], axis=1)
    landed = lax.all_to_all(leaving, axes, split_axis=0, concat_axis=0, tiled=True)
    arrived = landed[:, :ghosts].reshape(devices * ghosts, dwidth)
    top_boxes = landed[:, ghosts:, :ewidth].reshape(-1, ewidth)
    top_hot = top_lists == lax.broadcasted_iota(jnp.int32, (1, top_boxes.shape[0]), 1)
    top_picked = jnp.dot(top_hot.astype(BF), top_boxes, preferred_element_type=F32).astype(BF)

    dens_pool = jnp.concatenate([densities, arrived.T], axis=1)
    mult_pool = jnp.einsum("dl,de->el", dens_pool, p2m, preferred_element_type=F32).astype(BF)
    far, top_far = far_call(
        far_lists,
        m2l_rows,
        mult_pool,
        top_picked.reshape(offset_count // BLOCK, 1, BLOCK * ewidth),
    )
    near = near_call(near_lists, p2p_rows, dens_pool)

    local_exp = top_far.T.astype(BF)
    leaf_far = None
    for level_index in range(LEVELS):
        child_exp = jnp.einsum(
            "eb,kef->fbk", local_exp, l2l, preferred_element_type=F32
        ).reshape(ewidth, -1)
        if level_index < LEVELS - 1:
            local_exp = child_exp.astype(BF)
        else:
            leaf_far = child_exp
    leaf_local = (leaf_far + far).astype(BF)
    return near + jnp.einsum("el,ed->dl", leaf_local, l2p, preferred_element_type=F32)


def solution(mesh):
    in_specs = (
        P(None, ("curve", "sub")),
        P(None, ("curve", "sub")),
        P(None, ("curve", "sub")),
        P(("curve", "sub")),
        P(None, ("curve", "sub")),
        P(),
        P(),
        P(),
        P(),
        P(),
        P(),
    )
    out_specs = P(None, ("curve", "sub"))
    return jax.shard_map(shards, mesh=mesh, in_specs=in_specs, out_specs=out_specs, check_vma=False)
```

```python
import functools
import math

import jax
import jax.numpy as jnp
from jax import lax
from jax.experimental import pallas as pl
from jax.experimental.pallas import tpu as pltpu
from jax.sharding import PartitionSpec as P

LEVELS = 3
BLOCK = 8
BF = jnp.bfloat16
F32 = jnp.float32
F8 = jnp.float8_e4m3fn


def one_hot(row, depth):
    shape = (depth, row.shape[1])
    key = jnp.broadcast_to(row.astype(jnp.int16), shape)
    ids = lax.broadcasted_iota(jnp.int16, shape, 0)
    return jnp.where(key == ids, jnp.ones(shape, BF), jnp.zeros(shape, BF)).astype(F8)


def pick(pool, back, row):
    both = jnp.dot(pool[...], one_hot(row, pool.shape[1]), preferred_element_type=F32)
    width = both.shape[0] // 2
    return (both[:width] + both[width:]) * back[...]


def split(pool):
    values = pool.astype(F32)
    largest = jnp.maximum(jnp.max(jnp.abs(values), axis=1, keepdims=True), 1e-30)
    unit = jnp.exp2(jnp.floor(jnp.log2(largest)) - 6.0)
    scaled = values / unit
    high = lax.reduce_precision(scaled, 8, 3)
    return jnp.concatenate([high, scaled - high], axis=0).astype(F8), unit


def dot_t(left, right):
    return lax.dot_general(left, right, (((0,), (0,)), ((), ())), preferred_element_type=F32)


def rows_kernel(width, period, lanes, flat, out, wide, placed):
    groups = wide.shape[0] // lanes
    odd = placed.shape[1] // groups
    wide[...] = flat[...].astype(F32)

    def line(at):
        return wide[pl.ds(at, groups, stride=lanes), :]

    for row in range(period):
        start, offset = divmod(row * width, 128)
        for low in range(0, width, 128):
            size = min(128, width - low)
            here = start + low // 128
            first = line(here)
            if offset:
                rest = line(here + 1) if offset + size > 128 else first
                first = jnp.concatenate([first[:, offset:], rest[:, :offset]], axis=1)
            placed[low // 128, pl.ds(row, groups, stride=odd), :] = first
    for low in range(0, width, 128):
        high = min(low + 128, width)
        if odd == period:
            out[:, low:high] = placed[low // 128, :, : high - low].astype(BF)
            continue
        for group in range(groups):
            run = placed[low // 128, pl.ds(group * odd, period), : high - low]
            out[group * period : (group + 1) * period, low:high] = run.astype(BF)


def as_rows(flat, width, groups):
    total = flat.shape[0]
    period = 128 // math.gcd(width, 128)
    lanes = width * period // 128
    odd = period + (period % 16 == 0)
    return pl.pallas_call(
        functools.partial(rows_kernel, width, period, lanes),
        grid=(pl.cdiv(total // (width * period), groups),),
        in_specs=[pl.BlockSpec((groups * lanes, 128), lambda i: (i, 0))],
        out_specs=pl.BlockSpec((groups * period, width), lambda i: (i, 0)),
        out_shape=jax.ShapeDtypeStruct((total // width, width), BF),
        scratch_shapes=[
            pltpu.VMEM((groups * lanes, 128), F32),
            pltpu.VMEM((pl.cdiv(width, 128), groups * odd, 128), F32),
        ],
        compiler_params=pltpu.CompilerParams(vmem_limit_bytes=48 * 2**20),
    )(flat.reshape(total // 128, 128))


def far_kernel(lists, m2l, pool, back, top, far, top_far, picked):
    ewidth = back.shape[0]

    @pl.when(pl.program_id(0) == 0)
    def _():
        far[...] = jnp.zeros_like(far)
        top_far[...] = jnp.zeros_like(top_far)

    @pl.loop(0, BLOCK // 2)
    def _(pair):
        both = []
        for half in range(2):
            both.append(pick(pool, back, lists[pl.ds(2 * pair + half, 1), :]))
        start = pl.multiple_of(pair * (2 * ewidth), 16)
        picked[pl.ds(start, 2 * ewidth), :] = jnp.concatenate(both, axis=0).astype(BF)

    far[...] += dot_t(m2l[...], picked[...])
    top_far[...] += jnp.dot(top[0], m2l[...], preferred_element_type=F32)


def far_call(far_lists, m2l_rows, pool, back, top):
    offsets, leaves = far_lists.shape
    ewidth = back.shape[0]
    rows = BLOCK * ewidth
    return pl.pallas_call(
        far_kernel,
        grid=(offsets // BLOCK,),
        in_specs=[
            pl.BlockSpec((BLOCK, leaves), lambda i: (i, 0)),
            pl.BlockSpec((rows, ewidth), lambda i: (i, 0)),
            pl.BlockSpec(pool.shape, lambda i: (0, 0)),
            pl.BlockSpec(back.shape, lambda i: (0, 0)),
            pl.BlockSpec((1, 1, rows), lambda i: (i, 0, 0)),
        ],
        out_specs=[
            pl.BlockSpec((ewidth, leaves), lambda i: (0, 0)),
            pl.BlockSpec((1, ewidth), lambda i: (0, 0)),
        ],
        out_shape=[
            jax.ShapeDtypeStruct((ewidth, leaves), F32),
            jax.ShapeDtypeStruct((1, ewidth), F32),
        ],
        scratch_shapes=[pltpu.VMEM((rows, leaves), BF)],
        compiler_params=pltpu.CompilerParams(vmem_limit_bytes=48 * 2**20),
    )(far_lists, m2l_rows, pool, back, top)


def near_kernel(lists, p2p, pool, back, own, out, picked):
    dwidth = back.shape[0]
    classes, leaves = lists.shape

    @pl.loop(0, classes)
    def _(c):
        found = pick(pool, back, lists[pl.ds(c, 1), :]).astype(BF)
        picked[pl.ds(pl.multiple_of(c * dwidth, 16), dwidth), :] = found

    picked[classes * dwidth :, :] = own[...]
    out[...] = dot_t(p2p[...], picked[...])


def near_call(near_lists, p2p_rows, pool, back, own):
    classes, leaves = near_lists.shape
    dwidth = own.shape[0]
    return pl.pallas_call(
        near_kernel,
        out_shape=jax.ShapeDtypeStruct((dwidth, leaves), F32),
        scratch_shapes=[pltpu.VMEM(((classes + 1) * dwidth, leaves), BF)],
        compiler_params=pltpu.CompilerParams(vmem_limit_bytes=48 * 2**20),
    )(near_lists, p2p_rows, pool, back, own)


def shards(
    densities,
    far_lists,
    near_lists,
    ghost_sends,
    top_lists,
    point_to_mult,
    mult_to_mult,
    mult_to_local,
    local_to_local,
    local_to_point,
    point_to_point,
):
    axes = ("curve", "sub")
    devices = lax.axis_size(axes)
    dwidth, leaf_count = densities.shape
    offset_count = far_lists.shape[0]
    near_count = near_lists.shape[0]
    ewidth = point_to_mult.shape[0] // dwidth
    p2m = point_to_mult.reshape(dwidth, ewidth)
    m2m = as_rows(mult_to_mult, ewidth, 48).reshape(8, ewidth, ewidth)
    m2l_rows = as_rows(mult_to_local, ewidth, 240)
    l2l = as_rows(local_to_local, ewidth, 48).reshape(8, ewidth, ewidth)
    l2p = local_to_point.reshape(ewidth, dwidth)
    p2p_rows = as_rows(point_to_point, dwidth, 864)

    sends = ghost_sends[:, None] == lax.broadcasted_iota(jnp.int32, (1, leaf_count), 1)
    packed = lax.dot_general(
        sends.astype(BF), densities, (((1,), (1,)), ((), ())), preferred_element_type=F32
    ).astype(BF)
    mult_rows = jnp.einsum("dl,de->le", densities, p2m, preferred_element_type=F32).astype(BF)
    level_mult = mult_rows.T
    for level_index in range(LEVELS):
        grouped = level_mult.reshape(ewidth, -1, 8)
        level_mult = jnp.einsum("ebk,kef->fb", grouped, m2m, preferred_element_type=F32).astype(BF)
    ghosts = ghost_sends.shape[0] // devices
    tops = jnp.pad(level_mult.T, ((0, 0), (0, dwidth - ewidth)))
    tops = jnp.broadcast_to(tops[None], (devices,) + tops.shape)
    leaving = jnp.concatenate([packed.reshape(devices, ghosts, dwidth), tops], axis=1)
    landed = lax.all_to_all(leaving, axes, split_axis=0, concat_axis=0, tiled=True)
    arrived = landed[:, :ghosts].reshape(devices * ghosts, dwidth)
    top_boxes = landed[:, ghosts:, :ewidth].reshape(-1, ewidth)
    top_hot = top_lists == lax.broadcasted_iota(jnp.int32, (1, top_boxes.shape[0]), 1)
    top_picked = jnp.dot(top_hot.astype(BF), top_boxes, preferred_element_type=F32).astype(BF)

    dens_pool = jnp.concatenate([densities, arrived.T], axis=1)
    mult_pool = jnp.einsum("dl,de->el", dens_pool, p2m, preferred_element_type=F32).astype(BF)
    far, top_far = far_call(
        far_lists,
        m2l_rows,
        *split(mult_pool),
        top_picked.reshape(offset_count // BLOCK, 1, BLOCK * ewidth),
    )
    near = near_call(near_lists, p2p_rows, *split(dens_pool), densities)

    local_exp = top_far.T.astype(BF)
    leaf_far = None
    for level_index in range(LEVELS):
        child_exp = jnp.einsum(
            "eb,kef->fbk", local_exp, l2l, preferred_element_type=F32
        ).reshape(ewidth, -1)
        if level_index < LEVELS - 1:
            local_exp = child_exp.astype(BF)
        else:
            leaf_far = child_exp
    leaf_local = (leaf_far + far).astype(BF)
    return near + jnp.einsum("el,ed->dl", leaf_local, l2p, preferred_element_type=F32)


def solution(mesh):
    in_specs = (
        P(None, ("curve", "sub")),
        P(None, ("curve", "sub")),
        P(None, ("curve", "sub")),
        P(("curve", "sub")),
        P(None, ("curve", "sub")),
        P(),
        P(),
        P(),
        P(),
        P(),
        P(),
    )
    out_specs = P(None, ("curve", "sub"))
    return jax.shard_map(shards, mesh=mesh, in_specs=in_specs, out_specs=out_specs, check_vma=False)
```

```python
import functools
import math

import jax
import jax.numpy as jnp
from jax import lax
from jax.experimental import pallas as pl
from jax.experimental.pallas import tpu as pltpu
from jax.sharding import PartitionSpec as P

LEVELS = 3
BLOCK = 8
BF = jnp.bfloat16
F32 = jnp.float32


def one_hot(row, depth):
    leaves = row.shape[1]
    shape = (128, leaves)
    key = jnp.broadcast_to((row & 127).astype(jnp.int16), shape)
    ids = lax.broadcasted_iota(jnp.int16, shape, 0)
    low = jnp.where(key == ids, jnp.ones(shape, BF), jnp.zeros(shape, BF))
    high = jnp.broadcast_to(row >> 7, (16, leaves))
    parts = []
    for tile in range(depth // 128):
        here = jnp.where(high == tile, 1.0, 0.0).astype(BF)
        parts += [low[at : at + 16] * here for at in range(0, 128, 16)]
    return jnp.concatenate(parts, axis=0)


def pick(pool, row):
    return jnp.dot(pool[...], one_hot(row, pool.shape[1]), preferred_element_type=F32)


def dot_t(left, right):
    return lax.dot_general(left, right, (((0,), (0,)), ((), ())), preferred_element_type=F32)


def rows_kernel(width, period, lanes, flat, out, wide, placed):
    groups = wide.shape[0] // lanes
    odd = placed.shape[1] // groups
    wide[...] = flat[...].astype(F32)

    def line(at):
        return wide[pl.ds(at, groups, stride=lanes), :]

    for row in range(period):
        start, offset = divmod(row * width, 128)
        for low in range(0, width, 128):
            size = min(128, width - low)
            here = start + low // 128
            first = line(here)
            if offset:
                rest = line(here + 1) if offset + size > 128 else first
                first = jnp.concatenate([first[:, offset:], rest[:, :offset]], axis=1)
            placed[low // 128, pl.ds(row, groups, stride=odd), :] = first
    for low in range(0, width, 128):
        high = min(low + 128, width)
        if odd == period:
            out[:, low:high] = placed[low // 128, :, : high - low].astype(BF)
            continue
        for group in range(groups):
            run = placed[low // 128, pl.ds(group * odd, period), : high - low]
            out[group * period : (group + 1) * period, low:high] = run.astype(BF)


def as_rows(flat, width, groups):
    total = flat.shape[0]
    period = 128 // math.gcd(width, 128)
    lanes = width * period // 128
    odd = period + (period % 16 == 0)
    return pl.pallas_call(
        functools.partial(rows_kernel, width, period, lanes),
        grid=(pl.cdiv(total // (width * period), groups),),
        in_specs=[pl.BlockSpec((groups * lanes, 128), lambda i: (i, 0))],
        out_specs=pl.BlockSpec((groups * period, width), lambda i: (i, 0)),
        out_shape=jax.ShapeDtypeStruct((total // width, width), BF),
        scratch_shapes=[
            pltpu.VMEM((groups * lanes, 128), F32),
            pltpu.VMEM((pl.cdiv(width, 128), groups * odd, 128), F32),
        ],
        compiler_params=pltpu.CompilerParams(vmem_limit_bytes=48 * 2**20),
    )(flat.reshape(total // 128, 128))


def far_kernel(lists, m2l, pool, top, far, top_far, picked):
    ewidth = pool.shape[0]

    @pl.when(pl.program_id(0) == 0)
    def _():
        far[...] = jnp.zeros_like(far)
        top_far[...] = jnp.zeros_like(top_far)

    @pl.loop(0, BLOCK // 2)
    def _(pair):
        both = []
        for half in range(2):
            both.append(pick(pool, lists[pl.ds(2 * pair + half, 1), :]))
        start = pl.multiple_of(pair * (2 * ewidth), 16)
        picked[pl.ds(start, 2 * ewidth), :] = jnp.concatenate(both, axis=0).astype(BF)

    far[...] += dot_t(m2l[...], picked[...])
    top_far[...] += jnp.dot(top[0], m2l[...], preferred_element_type=F32)


def far_call(far_lists, m2l_rows, pool, top):
    offsets, leaves = far_lists.shape
    ewidth = pool.shape[0]
    rows = BLOCK * ewidth
    return pl.pallas_call(
        far_kernel,
        grid=(offsets // BLOCK,),
        in_specs=[
            pl.BlockSpec((BLOCK, leaves), lambda i: (i, 0)),
            pl.BlockSpec((rows, ewidth), lambda i: (i, 0)),
            pl.BlockSpec(pool.shape, lambda i: (0, 0)),
            pl.BlockSpec((1, 1, rows), lambda i: (i, 0, 0)),
        ],
        out_specs=[
            pl.BlockSpec((ewidth, leaves), lambda i: (0, 0)),
            pl.BlockSpec((1, ewidth), lambda i: (0, 0)),
        ],
        out_shape=[
            jax.ShapeDtypeStruct((ewidth, leaves), F32),
            jax.ShapeDtypeStruct((1, ewidth), F32),
        ],
        scratch_shapes=[pltpu.VMEM((rows, leaves), BF)],
        compiler_params=pltpu.CompilerParams(vmem_limit_bytes=48 * 2**20),
    )(far_lists, m2l_rows, pool, top)


def near_kernel(lists, p2p, pool, own, out, picked):
    dwidth = pool.shape[0]
    classes, leaves = lists.shape

    @pl.loop(0, classes)
    def _(c):
        found = pick(pool, lists[pl.ds(c, 1), :]).astype(BF)
        picked[pl.ds(pl.multiple_of(c * dwidth, 16), dwidth), :] = found

    picked[classes * dwidth :, :] = own[...]
    out[...] = dot_t(p2p[...], picked[...])


def near_call(near_lists, p2p_rows, pool, own):
    classes, leaves = near_lists.shape
    dwidth = own.shape[0]
    return pl.pallas_call(
        near_kernel,
        out_shape=jax.ShapeDtypeStruct((dwidth, leaves), F32),
        scratch_shapes=[pltpu.VMEM(((classes + 1) * dwidth, leaves), BF)],
        compiler_params=pltpu.CompilerParams(vmem_limit_bytes=48 * 2**20),
    )(near_lists, p2p_rows, pool, own)


def shards(
    densities,
    far_lists,
    near_lists,
    ghost_sends,
    top_lists,
    point_to_mult,
    mult_to_mult,
    mult_to_local,
    local_to_local,
    local_to_point,
    point_to_point,
):
    axes = ("curve", "sub")
    devices = lax.axis_size(axes)
    dwidth, leaf_count = densities.shape
    offset_count = far_lists.shape[0]
    near_count = near_lists.shape[0]
    ewidth = point_to_mult.shape[0] // dwidth
    p2m = point_to_mult.reshape(dwidth, ewidth)
    m2m = as_rows(mult_to_mult, ewidth, 48).reshape(8, ewidth, ewidth)
    m2l_rows = as_rows(mult_to_local, ewidth, 240)
    l2l = as_rows(local_to_local, ewidth, 48).reshape(8, ewidth, ewidth)
    l2p = local_to_point.reshape(ewidth, dwidth)
    p2p_rows = as_rows(point_to_point, dwidth, 864)

    sends = ghost_sends[:, None] == lax.broadcasted_iota(jnp.int32, (1, leaf_count), 1)
    packed = lax.dot_general(
        sends.astype(BF), densities, (((1,), (1,)), ((), ())), preferred_element_type=F32
    ).astype(BF)
    mult_rows = jnp.einsum("dl,de->le", densities, p2m, preferred_element_type=F32).astype(BF)
    level_mult = mult_rows.T
    for level_index in range(LEVELS):
        grouped = level_mult.reshape(ewidth, -1, 8)
        level_mult = jnp.einsum("ebk,kef->fb", grouped, m2m, preferred_element_type=F32).astype(BF)
    ghosts = ghost_sends.shape[0] // devices
    own_tops = level_mult.shape[1]
    span = ghosts + 8 * pl.cdiv(own_tops, 8)
    tops = jnp.pad(level_mult.T, ((0, span - ghosts - own_tops), (0, dwidth - ewidth)))
    tops = jnp.broadcast_to(tops[None], (devices,) + tops.shape)
    leaving = jnp.concatenate([packed.reshape(devices, ghosts, dwidth), tops], axis=1)
    landed = lax.all_to_all(leaving, axes, split_axis=0, concat_axis=0, tiled=True)
    landed = landed.reshape(devices * span, dwidth)
    slot = lax.broadcasted_iota(jnp.int32, (devices * span, 1), 0)
    ghost = lax.broadcasted_iota(jnp.int32, (1, devices * ghosts), 1)
    wanted = slot == ghost // ghosts * span + ghost % ghosts
    arrived = dot_t(landed, wanted.astype(BF)).astype(BF)
    top_at = top_lists // own_tops * span + ghosts + top_lists % own_tops
    top_hot = top_at == lax.broadcasted_iota(jnp.int32, (1, devices * span), 1)
    top_picked = jnp.dot(top_hot.astype(BF), landed[:, :ewidth], preferred_element_type=F32)
    top_picked = top_picked.astype(BF)

    dens_pool = jnp.concatenate([densities, arrived], axis=1)
    mult_pool = jnp.einsum("dl,de->el", dens_pool, p2m, preferred_element_type=F32).astype(BF)
    far, top_far = far_call(
        far_lists,
        m2l_rows,
        mult_pool,
        top_picked.reshape(offset_count // BLOCK, 1, BLOCK * ewidth),
    )
    near = near_call(near_lists, p2p_rows, dens_pool, densities)

    local_exp = top_far.T.astype(BF)
    leaf_far = None
    for level_index in range(LEVELS):
        child_exp = jnp.einsum(
            "eb,kef->fbk", local_exp, l2l, preferred_element_type=F32
        ).reshape(ewidth, -1)
        if level_index < LEVELS - 1:
            local_exp = child_exp.astype(BF)
        else:
            leaf_far = child_exp
    leaf_local = (leaf_far + far).astype(BF)
    return near + jnp.einsum("el,ed->dl", leaf_local, l2p, preferred_element_type=F32)


def solution(mesh):
    in_specs = (
        P(None, ("curve", "sub")),
        P(None, ("curve", "sub")),
        P(None, ("curve", "sub")),
        P(("curve", "sub")),
        P(None, ("curve", "sub")),
        P(),
        P(),
        P(),
        P(),
        P(),
        P(),
    )
    out_specs = P(None, ("curve", "sub"))
    return jax.shard_map(shards, mesh=mesh, in_specs=in_specs, out_specs=out_specs, check_vma=False)
```

```python
import functools
import math

import jax
import jax.numpy as jnp
from jax import lax
from jax.experimental import pallas as pl
from jax.experimental.pallas import tpu as pltpu
from jax.sharding import PartitionSpec as P

LEVELS = 3
BLOCK = 40
BF = jnp.bfloat16
F32 = jnp.float32


def one_hot(row, depth):
    leaves = row.shape[1]
    shape = (128, leaves)
    key = jnp.broadcast_to((row & 127).astype(jnp.int16), shape)
    ids = lax.broadcasted_iota(jnp.int16, shape, 0)
    low = jnp.where(key == ids, jnp.ones(shape, BF), jnp.zeros(shape, BF))
    high = jnp.broadcast_to(row >> 7, (16, leaves))
    parts = []
    for tile in range(depth // 128):
        here = jnp.where(high == tile, 1.0, 0.0).astype(BF)
        parts += [low[at : at + 16] * here for at in range(0, 128, 16)]
    return jnp.concatenate(parts, axis=0)


def pick(pool, row):
    parts = []
    for at in range(0, row.shape[1], 256):
        hot = one_hot(row[:, at : at + 256], pool.shape[1])
        parts.append(jnp.dot(pool[...], hot, preferred_element_type=F32))
    return jnp.concatenate(parts, axis=1)


def dot_t(left, right):
    return lax.dot_general(left, right, (((0,), (0,)), ((), ())), preferred_element_type=F32)


def rows_kernel(width, period, lanes, flat, out, wide, placed):
    groups = wide.shape[0] // lanes
    odd = placed.shape[1] // groups
    wide[...] = flat[...].astype(F32)

    def line(at):
        return wide[pl.ds(at, groups, stride=lanes), :]

    for row in range(period):
        start, offset = divmod(row * width, 128)
        for low in range(0, width, 128):
            size = min(128, width - low)
            here = start + low // 128
            first = line(here)
            if offset:
                rest = line(here + 1) if offset + size > 128 else first
                first = jnp.concatenate([first[:, offset:], rest[:, :offset]], axis=1)
            placed[low // 128, pl.ds(row, groups, stride=odd), :] = first
    for low in range(0, width, 128):
        high = min(low + 128, width)
        if odd == period:
            out[:, low:high] = placed[low // 128, :, : high - low].astype(BF)
            continue
        for group in range(groups):
            run = placed[low // 128, pl.ds(group * odd, period), : high - low]
            out[group * period : (group + 1) * period, low:high] = run.astype(BF)


def as_rows(flat, width, groups):
    total = flat.shape[0]
    period = 128 // math.gcd(width, 128)
    lanes = width * period // 128
    odd = period + (period % 16 == 0)
    return pl.pallas_call(
        functools.partial(rows_kernel, width, period, lanes),
        grid=(pl.cdiv(total // (width * period), groups),),
        in_specs=[pl.BlockSpec((groups * lanes, 128), lambda i: (i, 0))],
        out_specs=pl.BlockSpec((groups * period, width), lambda i: (i, 0)),
        out_shape=jax.ShapeDtypeStruct((total // width, width), BF),
        scratch_shapes=[
            pltpu.VMEM((groups * lanes, 128), F32),
            pltpu.VMEM((pl.cdiv(width, 128), groups * odd, 128), F32),
        ],
        compiler_params=pltpu.CompilerParams(vmem_limit_bytes=48 * 2**20),
    )(flat.reshape(total // 128, 128))


def far_kernel(lists, m2l, pool, top, far, top_far, picked):
    ewidth = pool.shape[0]

    @pl.when(pl.program_id(0) == 0)
    def _():
        far[...] = jnp.zeros_like(far)
        top_far[...] = jnp.zeros_like(top_far)

    @pl.loop(0, BLOCK // 2)
    def _(pair):
        both = []
        for half in range(2):
            both.append(pick(pool, lists[pl.ds(2 * pair + half, 1), :]))
        start = pl.multiple_of(pair * (2 * ewidth), 16)
        picked[pl.ds(start, 2 * ewidth), :] = jnp.concatenate(both, axis=0).astype(BF)

    for at in range(0, far.shape[1], 256):
        far[:, at : at + 256] += dot_t(m2l[...], picked[:, at : at + 256])
    top_far[...] += jnp.dot(top[0], m2l[...], preferred_element_type=F32)


def far_call(far_lists, m2l_rows, pool, top):
    offsets, leaves = far_lists.shape
    ewidth = pool.shape[0]
    rows = BLOCK * ewidth
    return pl.pallas_call(
        far_kernel,
        grid=(offsets // BLOCK,),
        in_specs=[
            pl.BlockSpec((BLOCK, leaves), lambda i: (i, 0)),
            pl.BlockSpec((rows, ewidth), lambda i: (i, 0)),
            pl.BlockSpec(pool.shape, lambda i: (0, 0)),
            pl.BlockSpec((1, 1, rows), lambda i: (i, 0, 0)),
        ],
        out_specs=[
            pl.BlockSpec((ewidth, leaves), lambda i: (0, 0)),
            pl.BlockSpec((1, ewidth), lambda i: (0, 0)),
        ],
        out_shape=[
            jax.ShapeDtypeStruct((ewidth, leaves), F32),
            jax.ShapeDtypeStruct((1, ewidth), F32),
        ],
        scratch_shapes=[pltpu.VMEM((rows, leaves), BF)],
        compiler_params=pltpu.CompilerParams(vmem_limit_bytes=48 * 2**20),
    )(far_lists, m2l_rows, pool, top)


def near_kernel(lists, p2p, pool, own, out, picked):
    dwidth = pool.shape[0]
    classes, leaves = lists.shape

    @pl.loop(0, classes)
    def _(c):
        found = pick(pool, lists[pl.ds(c, 1), :]).astype(BF)
        picked[pl.ds(pl.multiple_of(c * dwidth, 16), dwidth), :] = found

    picked[classes * dwidth :, :] = own[...]
    for at in range(0, leaves, 256):
        out[:, at : at + 256] = dot_t(p2p[...], picked[:, at : at + 256])


def near_call(near_lists, p2p_rows, pool, own):
    classes, leaves = near_lists.shape
    dwidth = own.shape[0]
    return pl.pallas_call(
        near_kernel,
        out_shape=jax.ShapeDtypeStruct((dwidth, leaves), F32),
        scratch_shapes=[pltpu.VMEM(((classes + 1) * dwidth, leaves), BF)],
        compiler_params=pltpu.CompilerParams(vmem_limit_bytes=48 * 2**20),
    )(near_lists, p2p_rows, pool, own)


def shards(
    densities,
    far_lists,
    near_lists,
    ghost_sends,
    top_lists,
    point_to_mult,
    mult_to_mult,
    mult_to_local,
    local_to_local,
    local_to_point,
    point_to_point,
):
    axes = ("curve", "sub")
    devices = lax.axis_size(axes)
    dwidth, leaf_count = densities.shape
    offset_count = far_lists.shape[0]
    near_count = near_lists.shape[0]
    ewidth = point_to_mult.shape[0] // dwidth
    p2m = point_to_mult.reshape(dwidth, ewidth)
    m2m = as_rows(mult_to_mult, ewidth, 48).reshape(8, ewidth, ewidth)
    m2l_rows = as_rows(mult_to_local, ewidth, 240)
    l2l = as_rows(local_to_local, ewidth, 48).reshape(8, ewidth, ewidth)
    l2p = local_to_point.reshape(ewidth, dwidth)
    p2p_rows = as_rows(point_to_point, dwidth, 864)

    sends = ghost_sends[:, None] == lax.broadcasted_iota(jnp.int32, (1, leaf_count), 1)
    packed = lax.dot_general(
        sends.astype(BF), densities, (((1,), (1,)), ((), ())), preferred_element_type=F32
    ).astype(BF)
    mult_rows = jnp.einsum("dl,de->le", densities, p2m, preferred_element_type=F32).astype(BF)
    level_mult = mult_rows.T
    for level_index in range(LEVELS):
        grouped = level_mult.reshape(ewidth, -1, 8)
        level_mult = jnp.einsum("ebk,kef->fb", grouped, m2m, preferred_element_type=F32).astype(BF)
    ghosts = ghost_sends.shape[0] // devices
    own_tops = level_mult.shape[1]
    span = ghosts + 8 * pl.cdiv(own_tops, 8)
    tops = jnp.pad(level_mult.T, ((0, span - ghosts - own_tops), (0, dwidth - ewidth)))
    tops = jnp.broadcast_to(tops[None], (devices,) + tops.shape)
    leaving = jnp.concatenate([packed.reshape(devices, ghosts, dwidth), tops], axis=1)
    landed = lax.all_to_all(leaving, axes, split_axis=0, concat_axis=0, tiled=True)
    landed = landed.reshape(devices * span, dwidth)
    slot = lax.broadcasted_iota(jnp.int32, (devices * span, 1), 0)
    ghost = lax.broadcasted_iota(jnp.int32, (1, devices * ghosts), 1)
    wanted = slot == ghost // ghosts * span + ghost % ghosts
    arrived = dot_t(landed, wanted.astype(BF)).astype(BF)
    top_at = top_lists // own_tops * span + ghosts + top_lists % own_tops
    top_hot = top_at == lax.broadcasted_iota(jnp.int32, (1, devices * span), 1)
    top_picked = jnp.dot(top_hot.astype(BF), landed[:, :ewidth], preferred_element_type=F32)
    top_picked = top_picked.astype(BF)

    dens_pool = jnp.concatenate([densities, arrived], axis=1)
    mult_pool = jnp.einsum("dl,de->el", dens_pool, p2m, preferred_element_type=F32).astype(BF)
    far, top_far = far_call(
        far_lists,
        m2l_rows,
        mult_pool,
        top_picked.reshape(offset_count // BLOCK, 1, BLOCK * ewidth),
    )
    near = near_call(near_lists, p2p_rows, dens_pool, densities)

    local_exp = top_far.T.astype(BF)
    leaf_far = None
    for level_index in range(LEVELS):
        child_exp = jnp.einsum(
            "eb,kef->fbk", local_exp, l2l, preferred_element_type=F32
        ).reshape(ewidth, -1)
        if level_index < LEVELS - 1:
            local_exp = child_exp.astype(BF)
        else:
            leaf_far = child_exp
    leaf_local = (leaf_far + far).astype(BF)
    return near + jnp.einsum("el,ed->dl", leaf_local, l2p, preferred_element_type=F32)


def solution(mesh):
    in_specs = (
        P(None, ("curve", "sub")),
        P(None, ("curve", "sub")),
        P(None, ("curve", "sub")),
        P(("curve", "sub")),
        P(None, ("curve", "sub")),
        P(),
        P(),
        P(),
        P(),
        P(),
        P(),
    )
    out_specs = P(None, ("curve", "sub"))
    return jax.shard_map(shards, mesh=mesh, in_specs=in_specs, out_specs=out_specs, check_vma=False)
```
